512 devices in a mesh: gx: 32 (over x_hi, y, core), gy: 16 (over x_lo, z).
Axes of the slice: x: 4 (x_hi: 2, x_lo: 2; x = x_hi * 2 + x_lo), y: 8, z: 8, core: 2. Of those that a mesh axis runs over, the one named last changes fastest.
Arguments:
- tokens: bfloat16 [256, 18432], P('gy', 'gx'), may hold values from -6 to 6
- gate_weight: bfloat16 [18432, 9216], P('gx', 'gy'), may hold values from -0.046875 to 0.046875
- up_weight: bfloat16 [18432, 9216], P('gx', 'gy'), may hold values from -0.046875 to 0.046875
- down_weight: bfloat16 [9216, 18432], P('gy', 'gx'), may hold values from -0.0625 to 0.0625
- cotangent: bfloat16 [256, 18432], P('gy', 'gx'), may hold values from -2.796875 to 2.796875
Outputs:
- output: bfloat16 [256, 18432], P('gy', 'gx')
- input_grad: bfloat16 [256, 18432], P('gy', 'gx')
- gate_grad: bfloat16 [18432, 9216], P('gx', 'gy')
- up_grad: bfloat16 [18432, 9216], P('gx', 'gy')
- down_grad: bfloat16 [9216, 18432], P('gy', 'gx')
The draws below stay inside these ranges and needn't reach their ends.
All inputs are finite; a program needn't handle non-finite values.
Results may differ from the reference program's by a relative error of at most 0.0049.
Values may be sent and summed in bfloat16 or wider, within the bound.
A program may use at most 64 MiB of HBM per device.

```python
import jax
import jax.numpy as jnp
from jax import lax

D = 18432
FF = 9216
TOKENS = 256


def with_spikes(values, key, source, target, shards_of, factor):
    owner, partner = [(jnp.arange(values.shape[dim]) // (values.shape[dim] // shards_of)).reshape([-1 if axis == dim else 1 for axis in range(values.ndim)]) for dim in (source, target)]
    chosen = jax.random.permutation(key, shards_of)[partner]
    strong = (owner == chosen) | (owner == (partner + shards_of // 2) % shards_of)
    return jnp.where(strong, factor * values, values)


def level_of(rng, dims, pieces, least, largest):
    gain = 1.0
    for position, shards_of in pieces:
        heights = jax.random.uniform(jax.random.fold_in(jax.random.fold_in(rng, 6), position), (shards_of,), jnp.float32, least / len(pieces), largest / len(pieces))
        gain = gain * jnp.repeat(jnp.exp(heights), dims[position] // shards_of).reshape((-1,) + (1,) * (len(dims) - 1 - position))
    return gain


def bell_draw(stream_key, extent, width, limit, pieces=(), dtype=jnp.bfloat16):
    array = width * jax.random.normal(stream_key, extent, jnp.float32)
    if pieces:
        array = array * level_of(stream_key, extent, pieces, -0.22, 0.18)
    return jnp.clip(array, -limit, limit).astype(dtype)


def noise_with(key, shape, spread, limit, shards, heavy, kind=jnp.bfloat16):
    array = spread * jax.random.normal(key, shape, jnp.float32)
    if shards:
        array = array * level_of(key, shape, shards, -0.22, 0.18)
    return jnp.clip(with_spikes(array, jax.random.fold_in(key, 3), *heavy), -limit, limit).astype(kind)


def setup_inputs(seed: int = 0) -> dict:
    key_of = jax.random.split(jax.random.key(seed), 6)
    return {
        "tokens": noise_with(key_of[0], (TOKENS, D), 1.0, 6.0, ((0, 16), (1, 32)), (1, 0, 32, 2.75)),
        "gate_weight": bell_draw(key_of[1], (D, FF), D ** -0.5, 0.046875, ((0, 32), (1, 16))),
        "up_weight": bell_draw(key_of[2], (D, FF), D ** -0.5, 0.046875, ((0, 32), (1, 16))),
        "down_weight": bell_draw(key_of[3], (FF, D), FF ** -0.5, 0.0625, ((0, 16), (1, 32))),
        "cotangent": noise_with(key_of[4], (TOKENS, D), 0.35, 2.796875, ((0, 16), (1, 32)), (1, 0, 32, 2.75)),
    }


def contract_last(left, right):
    return lax.dot_general(left, right, (((1,), (1,)), ((), ())), preferred_element_type=jnp.float32)


def contract_first(left, right):
    return lax.dot_general(left, right, (((0,), (0,)), ((), ())), preferred_element_type=jnp.float32)


def reference(tokens, gate_weight, up_weight, down_weight, cotangent):
    gate = jnp.dot(tokens, gate_weight, preferred_element_type=jnp.float32)
    up = jnp.dot(tokens, up_weight, preferred_element_type=jnp.float32)
    sigmoid_gate = jax.nn.sigmoid(gate)
    activated = gate * sigmoid_gate
    hidden = (activated * up).astype(jnp.bfloat16)
    output = jnp.dot(hidden, down_weight, preferred_element_type=jnp.float32).astype(jnp.bfloat16)
    hidden_grad = contract_last(cotangent, down_weight)
    gate_delta = (hidden_grad * up * sigmoid_gate * (1.0 + gate * (1.0 - sigmoid_gate))).astype(jnp.bfloat16)
    up_delta = (hidden_grad * activated).astype(jnp.bfloat16)
    input_grad = (contract_last(gate_delta, gate_weight) + contract_last(up_delta, up_weight)).astype(jnp.bfloat16)
    gate_grad = contract_first(tokens, gate_delta).astype(jnp.bfloat16)
    up_grad = contract_first(tokens, up_delta).astype(jnp.bfloat16)
    down_grad = contract_first(hidden, cotangent).astype(jnp.bfloat16)
    return (output, input_grad, gate_grad, up_grad, down_grad)
```

```python
import jax
import jax.numpy as jnp
from jax import lax
from jax.experimental import pallas as pl
from jax.experimental.pallas import tpu as pltpu
from jax.sharding import PartitionSpec as P

MESH = pl.DeviceIdType.MESH
F32 = jnp.float32
BF16 = jnp.bfloat16


def mm(a, b):
    return lax.dot_general(a, b, (((1,), (0,)), ((), ())), preferred_element_type=F32)


def mm_nt(a, b):
    return lax.dot_general(a, b, (((1,), (1,)), ((), ())), preferred_element_type=F32)


def mm_tn(a, b):
    return lax.dot_general(a, b, (((0,), (0,)), ((), ())), preferred_element_type=F32)


def each(start, stop, body):
    def step(i, carry):
        body(i)
        return carry

    lax.fori_loop(start, stop, step, 0)


def kernel(
    tok, wg, wu, wd, cot,
    out, ig, gate_grad, up_grad, down_grad,
    mine, w, xt, xc, xw, part, sgu, shg, rgu, rhg, gh, gd, ghp, gdp, so, si, ro, ri,
    lsem, wss, wrs, tss, trs, css, crs, guss, gurs, hgss, hgrs, hss, hrs, dss, drs,
    oss, ors, iss, irs, fss, frs,
):
    gx, gy = lax.axis_index("gx"), lax.axis_index("gy")
    q, c = lax.div(gx, 2), lax.rem(gx, 2)
    xh, y = lax.div(q, 8), lax.rem(q, 8)
    xl, z = lax.div(gy, 8), lax.rem(gy, 8)
    other = 1 - c
    peer = (q * 2 + other, gy)

    def row_chip(i):
        t = lax.rem(xh + lax.div(i, 8), 2) * 8 + lax.rem(y + i, 8)
        return t, (t * 2 + c, gy)

    def col_dev(i, core):
        return (q * 2 + core, lax.rem(xl + lax.div(i, 8), 2) * 8 + lax.rem(z + i, 8))

    def remote(src, dst, ssem, rsem, dev):
        return pltpu.make_async_remote_copy(
            src_ref=src, dst_ref=dst, send_sem=ssem, recv_sem=rsem, device_id=dev, device_id_type=MESH
        )

    loads = [
        pltpu.make_async_copy(src, dst, lsem.at[n])
        for n, (src, dst) in enumerate(
            [
                (tok, mine.at[0]), (cot, mine.at[1]),
                (wg, w.at[c, 0]), (wu, w.at[c, 1]), (wd, w.at[c, 2]),
            ]
        )
    ]
    for copy in loads:
        copy.start()

    barrier = pltpu.get_barrier_semaphore()

    def greet(dev):
        pl.semaphore_signal(barrier, inc=1, device_id=dev, device_id_type=MESH)

    each(1, 16, lambda i: greet(row_chip(i)[1]))

    def greet_col(i):
        greet(col_dev(i, xl))

        @pl.when(lax.rem(xl + lax.div(i, 8), 2) == c)
        def _():
            greet(col_dev(i, 1 - xl))

    each(1, 16, greet_col)
    greet(peer)
    pl.semaphore_wait(barrier, 15 + 15 + 8 - jnp.where(xl == c, 1, 0) + 1)

    loads[0].wait()
    loads[1].wait()

    def gather(n, dst, ss, rs):
        view = dst.at[c, pl.ds(pl.multiple_of(z * 16, 16), 16)]

        def desc(i):
            return remote(mine.at[n], view, ss.at[i], rs.at[c * 8 + z], col_dev(i, xl))

        def start():
            @pl.when(c == xl)
            def _():
                pltpu.make_async_copy(mine.at[n], view, rs.at[c * 8 + z]).start()

            @pl.when(c != xl)
            def _():
                desc(0).start()

            each(1, 16, lambda i: desc(i).start())

        def finish():
            @pl.when(c != xl)
            def _():
                desc(0).wait_send()

            each(1, 16, lambda i: desc(i).wait_send())

        def arrive():
            def one(s):
                rows = pl.ds(pl.multiple_of(lax.rem(s, 8) * 16, 16), 16)
                remote(mine.at[n], dst.at[lax.div(s, 8), rows], ss.at[0], rs.at[s], peer).wait_recv()

            each(0, 16, one)

        return start, finish, arrive

    tok_start, tok_finish, tok_arrive = gather(0, xt, tss, trs)
    cot_start, cot_finish, cot_arrive = gather(1, xc, css, crs)
    tok_start()
    wcopies = [
        remote(src, w.at[c, n], wss.at[n], wrs.at[n], peer) for n, src in enumerate((wg, wu, wd))
    ]
    for copy in wcopies:
        copy.start()
    cot_start()
    for copy in loads[2:]:
        copy.wait()
    wcopies[0].wait_recv()
    wcopies[1].wait_recv()

    def scatter(src, dst, ss, rs):
        def desc(i):
            t, dev = row_chip(i)
            return remote(src.at[t], dst.at[i], ss.at[i], rs.at[i], dev)

        return (
            lambda: each(1, 16, lambda i: desc(i).start()),
            lambda: each(1, 16, lambda i: desc(i).wait_send()),
            lambda: each(1, 16, lambda i: desc(i).wait_recv()),
        )

    gu_start, gu_finish, gu_arrive = scatter(sgu, rgu, guss, gurs)
    hg_start, hg_finish, hg_arrive = scatter(shg, rhg, hgss, hgrs)

    tok_arrive()
    for n in range(2):
        p = (mm(xt[0], w[0, n]) + mm(xt[1], w[1, n])).reshape(16, 8, 576)
        part[n] = p
        sgu[:, n] = p.astype(BF16)
    gu_start()
    wcopies[2].wait_recv()
    cot_arrive()
    p = (mm_nt(xc[0], w[0, 2]) + mm_nt(xc[1], w[1, 2])).reshape(16, 8, 576)
    part[2] = p
    shg[...] = p.astype(BF16)
    hg_start()

    fwd = [
        remote(xt.at[other], xw.at[0], fss.at[0], frs.at[0], peer),
        remote(xc.at[other], xw.at[1], fss.at[1], frs.at[1], peer),
        remote(gh, ghp, fss.at[2], frs.at[2], peer),
        remote(gd, gdp, fss.at[3], frs.at[3], peer),
    ]
    fwd[0].start()
    fwd[1].start()

    def spread(buf, ss, rs):
        def desc(i):
            return remote(buf.at[q], buf.at[q], ss.at[i], rs.at[i], row_chip(i)[1])

        return (
            lambda: each(1, 16, lambda i: desc(i).start()),
            lambda: each(1, 16, lambda i: desc(i).wait_send()),
            lambda: each(1, 16, lambda i: desc(i).wait_recv()),
        )

    h_start, h_finish, h_arrive = spread(gh, hss, hrs)
    d_start, d_finish, d_arrive = spread(gd, dss, drs)

    gu_arrive()
    gate, up = part[0, q], part[1, q]
    for i in range(1, 16):
        gate += rgu[i, 0].astype(F32)
        up += rgu[i, 1].astype(F32)
    sig = jax.nn.sigmoid(gate)
    act = gate * sig
    gh[q] = (act * up).astype(BF16)
    h_start()
    hg_arrive()
    hgrad = part[2, q]
    for i in range(1, 16):
        hgrad += rhg[i].astype(F32)
    gd[q, 0] = (hgrad * up * sig * (1.0 + gate * (1.0 - sig))).astype(BF16)
    gd[q, 1] = (hgrad * act).astype(BF16)
    d_start()

    def deliver(src, dst, ss, rs):
        slot = xl * 8 + z

        def dev_of(j):
            return (q * 2 + lax.div(j, 8), c * 8 + lax.rem(z + j, 8))

        def desc(j):
            rows = pl.ds(pl.multiple_of(lax.rem(z + j, 8) * 16, 16), 16)
            return remote(src.at[lax.div(j, 8), rows], dst.at[slot], ss.at[j], rs.at[slot], dev_of(j))

        def is_self(j):
            return (xl == c) & (j == c * 8)

        def start():
            def one(j):
                @pl.when(is_self(j))
                def _():
                    rows = pl.ds(pl.multiple_of(z * 16, 16), 16)
                    pltpu.make_async_copy(src.at[c, rows], dst.at[slot], rs.at[slot]).start()

                @pl.when(jnp.logical_not(is_self(j)))
                def _():
                    desc(j).start()

            each(0, 16, one)

        def finish():
            def one(j):
                @pl.when(jnp.logical_not(is_self(j)))
                def _():
                    desc(j).wait_send()

            each(0, 16, one)

        def arrive():
            def one(s):
                remote(src.at[0, pl.ds(0, 16)], dst.at[s], ss.at[0], rs.at[s], peer).wait_recv()

            each(0, 16, one)

        return start, finish, arrive

    o_start, o_finish, o_arrive = deliver(so, ro, oss, ors)
    i_start, i_finish, i_arrive = deliver(si, ri, iss, irs)

    h_arrive()
    fwd[2].start()
    hidden = gh[...].reshape(128, 576)
    for k in range(2):
        so[k] = mm(hidden, w[k, 2]).astype(BF16)
    o_start()
    fwd[0].wait_recv()
    fwd[1].wait_recv()
    fwd[2].wait_recv()
    down_grad[...] = (
        mm_tn(gh[...].reshape(128, 576), xc[c]) + mm_tn(ghp[...].reshape(128, 576), xw[1])
    ).astype(BF16)

    d_arrive()
    fwd[3].start()
    gdl, udl = gd[:, 0].reshape(128, 576), gd[:, 1].reshape(128, 576)
    for k in range(2):
        si[k] = (mm_nt(gdl, w[k, 0]) + mm_nt(udl, w[k, 1])).astype(BF16)
    i_start()
    fwd[3].wait_recv()
    for n, ref in enumerate((gate_grad, up_grad)):
        ref[...] = (
            mm_tn(xt[c], gd[:, n].reshape(128, 576)) + mm_tn(xw[0], gdp[:, n].reshape(128, 576))
        ).astype(BF16)

    def total(ref):
        t = ref[0].astype(F32)
        for s in range(1, 16):
            t += ref[s].astype(F32)
        return t.astype(BF16)

    o_arrive()
    out[...] = total(ro)
    i_arrive()
    ig[...] = total(ri)

    for copy in wcopies + fwd:
        copy.wait_send()
    for finish in (
        tok_finish, cot_finish, gu_finish, hg_finish, h_finish, d_finish, o_finish, i_finish
    ):
        finish()


def shards(tokens, gate_weight, up_weight, down_weight, cotangent):
    vmem = pl.BlockSpec(memory_space=pltpu.VMEM)
    hbm = pl.BlockSpec(memory_space=pl.ANY)
    dma = pltpu.SemaphoreType.DMA
    act = jax.ShapeDtypeStruct((16, 576), BF16)
    weight = jax.ShapeDtypeStruct((576, 576), BF16)
    return pl.pallas_call(
        kernel,
        out_shape=(act, act, weight, weight, weight),
        in_specs=[hbm] * 5,
        out_specs=(vmem,) * 5,
        scratch_shapes=[
            pltpu.VMEM((2, 16, 576), BF16),
            pltpu.VMEM((2, 3, 576, 576), BF16),
            pltpu.VMEM((2, 128, 576), BF16),
            pltpu.VMEM((2, 128, 576), BF16),
            pltpu.VMEM((2, 128, 576), BF16),
            pltpu.VMEM((3, 16, 8, 576), F32),
            pltpu.VMEM((16, 2, 8, 576), BF16),
            pltpu.VMEM((16, 8, 576), BF16),
            pltpu.VMEM((16, 2, 8, 576), BF16),
            pltpu.VMEM((16, 8, 576), BF16),
            pltpu.VMEM((16, 8, 576), BF16),
            pltpu.VMEM((16, 2, 8, 576), BF16),
            pltpu.VMEM((16, 8, 576), BF16),
            pltpu.VMEM((16, 2, 8, 576), BF16),
            pltpu.VMEM((2, 128, 576), BF16),
            pltpu.VMEM((2, 128, 576), BF16),
            pltpu.VMEM((16, 16, 576), BF16),
            pltpu.VMEM((16, 16, 576), BF16),
            dma((5,)),
            dma((3,)), dma((3,)),
        ]
        + [dma((16,))] * 16
        + [dma((4,))] * 2,
        compiler_params=pltpu.CompilerParams(
            collective_id=0, has_side_effects=True, vmem_limit_bytes=40 * 1024 * 1024
        ),
        cost_estimate=pl.CostEstimate(
            flops=9 * 2 * 256 * 576 * 576, bytes_accessed=6 * 576 * 576 * 2, transcendentals=8 * 576
        ),
    )(tokens, gate_weight, up_weight, down_weight, cotangent)


def solution(mesh):
    placed = (P("gy", "gx"), P("gx", "gy"), P("gx", "gy"), P("gy", "gx"), P("gy", "gx"))
    return jax.shard_map(
        shards,
        mesh=mesh,
        in_specs=placed,
        out_specs=(P("gy", "gx"), P("gy", "gx"), P("gx", "gy"), P("gx", "gy"), P("gy", "gx")),
        check_vma=False,
    )
```

```python
import jax
import jax.numpy as jnp
from jax import lax
from jax.experimental import pallas as pl
from jax.experimental.pallas import tpu as pltpu
from jax.sharding import PartitionSpec as P

MESH = pl.DeviceIdType.MESH
F32 = jnp.float32
BF16 = jnp.bfloat16


def mm(a, b):
    return lax.dot_general(a, b, (((1,), (0,)), ((), ())), preferred_element_type=F32)


def mm_tn(a, b):
    return lax.dot_general(a, b, (((0,), (0,)), ((), ())), preferred_element_type=F32)


def each(start, stop, body):
    def step(i, carry):
        body(i)
        return carry

    lax.fori_loop(start, stop, step, 0)


def kernel(
    tok, wg, wu, wd, cot,
    out, ig, gate_grad, up_grad, down_grad,
    mine, packed, w, wj, wt, wdt, xt, xc, xw, pgu, phg, sgu, shg, rgu, rhg, gh, gd, ghp, gdp, so, si, ro, ri, act_out, w_out,
    near, lsem, wsem, wss, wrs, tss, trs, css, crs, guss, gurs, hgss, hgrs, hss, hrs, dss, drs,
    oss, ors, iss, irs, fss, frs,
):
    gx, gy = lax.axis_index("gx"), lax.axis_index("gy")
    c = lax.rem(gx, 2)
    xh, y = lax.div(gx, 16), lax.rem(lax.div(gx, 2), 8)
    xl, z = lax.div(gy, 8), lax.rem(gy, 8)
    other = 1 - c
    me = y * 2 + xh

    def row_dev(dx, dy):
        return (lax.rem(xh + dx, 2) * 16 + lax.rem(y + dy + 8, 8) * 2 + c, gy)

    def col_dev(dx, dz, core):
        return (gx - c + core, lax.rem(xl + dx, 2) * 8 + lax.rem(z + dz + 8, 8))

    peer = col_dev(0, 0, other)

    def remote(src, dst, ssem, rsem, dev):
        return pltpu.make_async_remote_copy(
            src_ref=src, dst_ref=dst, send_sem=ssem, recv_sem=rsem, device_id=dev, device_id_type=MESH
        )

    loads = [
        pltpu.make_async_copy(src, dst, lsem.at[n])
        for n, (src, dst) in enumerate(
            [
                (tok, mine.at[0]), (cot, mine.at[1]),
                (wg, w.at[c, 0]), (wu, w.at[c, 1]), (wd, w.at[c, 2]),
            ]
        )
    ]
    for copy in loads:
        copy.start()

    def greet(sem):
        def one(i):
            dx, d = lax.div(i, 5), lax.rem(i, 5) - 2

            @pl.when(i != 2)
            def _():
                pl.semaphore_signal(sem, inc=1, device_id=row_dev(dx, d), device_id_type=MESH)
                pl.semaphore_signal(sem, inc=1, device_id=col_dev(dx, d, c), device_id_type=MESH)

            pl.semaphore_signal(sem, inc=1, device_id=col_dev(dx, d, other), device_id_type=MESH)

        each(0, 10, one)

    barrier = pltpu.get_barrier_semaphore()
    greet(barrier)
    pl.semaphore_wait(barrier, 28)

    loads[0].wait()
    loads[1].wait()
    for n in range(2):
        packed[n] = jnp.concatenate([mine[n, :8], mine[n, 8:]], axis=1)

    def gather(n, dst, ss, rs):
        slot = z * 2 + c

        def desc(i):
            dx, d = lax.div(i, 5), lax.rem(i, 5) - 2
            return remote(packed.at[n], dst.at[z, c], ss.at[i], rs.at[slot], col_dev(dx, d, xl))

        def local():
            return pltpu.make_async_copy(packed.at[n], dst.at[z, c], rs.at[slot])

        def start():
            @pl.when(c == xl)
            def _():
                local().start()

            def one(i):
                @pl.when((i != 2) | (c != xl))
                def _():
                    desc(i).start()

            each(0, 10, one)

        def ahead(side):
            zs = lax.rem(z - 2 * side + 8, 8)
            k = (1 - side) // 2
            third = remote(dst.at[zs], dst.at[zs], ss.at[10 + k], rs.at[16 + k], col_dev(0, side, c))
            fourth = remote(
                dst.at[zs, k], dst.at[zs, k], ss.at[12 + k], rs.at[18 + k], col_dev(0, 2 * side, c)
            )
            return zs, third, fourth

        def here(zs, k):
            remote(packed.at[n], dst.at[zs, k], ss.at[0], rs.at[zs * 2 + k], peer).wait_recv()

        def forward():
            for side in (1, -1):
                zs, third, fourth = ahead(side)
                here(zs, 0)
                here(zs, 1)
                third.start()
                fourth.start()

        def arrive():
            for d in (0, 1, -1):
                zs = lax.rem(z + d + 8, 8)
                here(zs, 0)
                here(zs, 1)
            for side in (1, -1):
                _, third, fourth = ahead(side)
                third.wait_recv()
                fourth.wait_recv()

        def finish():
            def one(i):
                @pl.when((i != 2) | (c != xl))
                def _():
                    desc(i).wait_send()

            each(0, 10, one)
            for side in (1, -1):
                _, third, fourth = ahead(side)
                third.wait_send()
                fourth.wait_send()

        return start, forward, arrive, finish

    tok_start, tok_forward, tok_arrive, tok_finish = gather(0, xt, tss, trs)
    cot_start, cot_forward, cot_arrive, cot_finish = gather(1, xc, css, crs)
    tok_start()
    cot_start()
    wcopies = [
        remote(src, w.at[c, n], wss.at[n], wrs.at[n], peer) for n, src in enumerate((wg, wu, wd))
    ]
    for copy in wcopies:
        copy.start()
    greet(near)
    tok_forward()
    cot_forward()
    for copy in loads[2:]:
        copy.wait()
    wcopies[0].wait_recv()
    wcopies[1].wait_recv()
    for k in range(2):
        wj[k] = jnp.concatenate([w[k, 0], w[k, 1]], axis=1)
    pl.semaphore_wait(near, 28)
    wcopies[2].wait_recv()
    for k in range(2):
        wdt[k] = w[k, 2].T
        wt[k] = jnp.concatenate([w[k, 0].T, w[k, 1].T], axis=0)

    def rows(x):
        x = x.reshape(64, 1152)
        return jnp.concatenate([x[:, :576], x[:, 576:]], axis=0)

    def shares(x):
        return jnp.concatenate([x[:64], x[64:]], axis=1).reshape(8, 8, 1152)

    def scatter(src, dst, ss, rs):
        def desc(i):
            dx, dy = lax.rem(i, 2), lax.div(i, 2)
            t = lax.rem(y + dy, 8) * 2 + lax.rem(xh + dx, 2)
            return remote(src.at[t], dst.at[i], ss.at[i], rs.at[i], row_dev(dx, dy))

        return (
            lambda: each(1, 16, lambda i: desc(i).start()),
            lambda: each(1, 16, lambda i: desc(i).wait_recv()),
            lambda: each(1, 16, lambda i: desc(i).wait_send()),
        )

    gu_start, gu_arrive, gu_finish = scatter(sgu, rgu, guss, gurs)
    hg_start, hg_arrive, hg_finish = scatter(shg, rhg, hgss, hgrs)

    tok_arrive()
    p = mm(rows(xt[:, 0]), wj[0]) + mm(rows(xt[:, 1]), wj[1])
    sgu[...] = p.reshape(16, 8, 1152).astype(BF16)
    gu_start()
    pgu[...] = p.reshape(16, 8, 1152)
    cot_arrive()
    p = mm(rows(xc[:, 0]), wdt[0]) + mm(rows(xc[:, 1]), wdt[1])
    shg[...] = p.reshape(16, 8, 576).astype(BF16)
    hg_start()
    phg[...] = p.reshape(16, 8, 576)

    fwd = [
        remote(xt.at[:, other], xw.at[0], fss.at[0], frs.at[0], peer),
        remote(xc.at[:, other], xw.at[1], fss.at[1], frs.at[1], peer),
        remote(gh, ghp, fss.at[2], frs.at[2], peer),
        remote(gd, gdp, fss.at[3], frs.at[3], peer),
    ]
    fwd[0].start()
    fwd[1].start()

    def spread(buf, ss, rs):
        def desc(i):
            return remote(
                buf.at[me], buf.at[me], ss.at[i], rs.at[me], row_dev(lax.div(i, 5), lax.rem(i, 5) - 2)
            )

        def near_one(i):
            @pl.when(i != 2)
            def _():
                desc(i).start()

        def pair(dy):
            return pl.ds(pl.multiple_of(lax.rem(y + dy + 8, 8) * 2, 2), 2)

        def here(dy):
            ys = lax.rem(y + dy + 8, 8)
            for k in range(2):
                remote(buf.at[me], buf.at[ys * 2 + k], ss.at[0], rs.at[ys * 2 + k], peer).wait_recv()

        def third(side):
            view = buf.at[pair(-2 * side)]
            k = (1 - side) // 2
            return remote(view, view, ss.at[10 + k], rs.at[16 + k], row_dev(0, side))

        def fourth():
            side = 1 - 2 * c
            view = buf.at[pair(-2 * side)]
            return remote(view, view, ss.at[12], rs.at[18], row_dev(0, 2 * side))

        def forward():
            for side in (1, -1):
                here(-2 * side)
                third(side).start()
            fourth().start()

        def arrive():
            remote(buf.at[me], buf.at[me], ss.at[0], rs.at[y * 2 + 1 - xh], peer).wait_recv()
            here(1)
            here(-1)
            third(1).wait_recv()
            third(-1).wait_recv()
            fourth().wait_recv()

        def finish():
            def one(i):
                @pl.when(i != 2)
                def _():
                    desc(i).wait_send()

            each(0, 10, one)
            third(1).wait_send()
            third(-1).wait_send()
            fourth().wait_send()

        return lambda: each(0, 10, near_one), forward, arrive, finish

    h_start, h_forward, h_arrive, h_finish = spread(gh, hss, hrs)
    d_start, d_forward, d_arrive, d_finish = spread(gd, dss, drs)

    gu_arrive()
    total = pgu[me]
    for i in range(1, 16):
        total += rgu[i].astype(F32)
    gate, up = total[:, :576], total[:, 576:]
    sig = jax.nn.sigmoid(gate)
    act = gate * sig
    gh[me] = (act * up).astype(BF16)
    h_start()
    slope = up * sig * (1.0 + gate * (1.0 - sig))
    both = jnp.concatenate([slope, act], axis=1)
    hg_arrive()
    hgrad = phg[me]
    for i in range(1, 16):
        hgrad += rhg[i].astype(F32)
    gd[me] = (jnp.concatenate([hgrad, hgrad], axis=1) * both).astype(BF16)
    d_start()
    h_forward()
    d_forward()

    def deliver(src, dst, ss, rs):
        slot = xl * 8 + z

        def desc(k, j):
            zt = lax.rem(z + j, 8)
            return remote(
                src.at[k, zt], dst.at[slot], ss.at[k * 8 + j], rs.at[slot], (gx - c + k, c * 8 + zt)
            )

        def is_self(k, j):
            return (xl == c) & (c == k) & (j == 0)

        def start(k):
            def one(j):
                @pl.when(is_self(k, j))
                def _():
                    pltpu.make_async_copy(src.at[k, z], dst.at[slot], rs.at[slot]).start()

                @pl.when(jnp.logical_not(is_self(k, j)))
                def _():
                    desc(k, j).start()

            each(0, 8, one)

        def arrive():
            each(
                0, 16, lambda s: remote(src.at[0, 0], dst.at[s], ss.at[0], rs.at[s], peer).wait_recv()
            )

        def finish():
            for k in range(2):

                def one(j):
                    @pl.when(jnp.logical_not(is_self(k, j)))
                    def _():
                        desc(k, j).wait_send()

                each(0, 8, one)

        return start, arrive, finish

    o_start, o_arrive, o_finish = deliver(so, ro, oss, ors)
    i_start, i_arrive, i_finish = deliver(si, ri, iss, irs)

    h_arrive()
    fwd[2].start()
    hidden = gh[...].reshape(128, 576)
    for k in range(2):
        so[k] = shares(mm(hidden, w[k, 2])).astype(BF16)
        o_start(k)
    for copy in fwd[:3]:
        copy.wait_recv()

    def own(x):
        return rows(x[:, pl.ds(c, 1)])

    stores = [
        pltpu.make_async_copy(src, dst, wsem.at[n])
        for n, (src, dst) in enumerate(
            [
                (act_out.at[0], out), (act_out.at[1], ig),
                (w_out.at[0], gate_grad), (w_out.at[1], up_grad), (w_out.at[2], down_grad),
            ]
        )
    ]
    w_out[2] = (
        mm_tn(gh[...].reshape(128, 576), own(xc)) + mm_tn(ghp[...].reshape(128, 576), rows(xw[1]))
    ).astype(BF16)
    stores[4].start()

    d_arrive()
    fwd[3].start()
    joined = gd[...].reshape(128, 1152)
    for k in range(2):
        si[k] = shares(mm(joined, wt[k])).astype(BF16)
        i_start(k)
    fwd[3].wait_recv()
    both = mm_tn(own(xt), gd[...].reshape(128, 1152)) + mm_tn(
        rows(xw[0]), gdp[...].reshape(128, 1152)
    )
    w_out[0] = both[:, :576].astype(BF16)
    w_out[1] = both[:, 576:].astype(BF16)
    stores[2].start()
    stores[3].start()

    def summed(ref):
        t = ref[0].astype(F32)
        for s in range(1, 16):
            t += ref[s].astype(F32)
        return jnp.concatenate([t[:, :576], t[:, 576:]], axis=0).astype(BF16)

    o_arrive()
    act_out[0] = summed(ro)
    stores[0].start()
    for copy in wcopies + fwd:
        copy.wait_send()
    for finish in (tok_finish, cot_finish, gu_finish, hg_finish, h_finish, d_finish, o_finish):
        finish()
    i_arrive()
    act_out[1] = summed(ri)
    stores[1].start()
    i_finish()
    for copy in stores:
        copy.wait()


def write_back(*refs):
    ins, outs, bufs, get, put = refs[:5], refs[5:10], refs[10:15], refs[15], refs[16]
    parts = [(n, slice(None)) for n in range(2)]
    parts += [(n, pl.ds(r * 192, 192)) for r in range(3) for n in range(2, 5)]
    reads = [pltpu.make_async_copy(ins[n].at[r], bufs[n].at[r], get.at[i]) for i, (n, r) in enumerate(parts)]
    writes = [pltpu.make_async_copy(bufs[n].at[r], outs[n].at[r], put.at[i]) for i, (n, r) in enumerate(parts)]
    for copy in reads:
        copy.start()
    for read, write in zip(reads, writes):
        read.wait()
        write.start()
    for copy in writes:
        copy.wait()


def shards(tokens, gate_weight, up_weight, down_weight, cotangent):
    hbm = pl.BlockSpec(memory_space=pltpu.HBM)
    dma = pltpu.SemaphoreType.DMA
    act = jax.ShapeDtypeStruct((16, 576), BF16)
    weight = jax.ShapeDtypeStruct((576, 576), BF16)
    results = pl.pallas_call(
        kernel,
        out_shape=(act, act, weight, weight, weight),
        in_specs=[hbm] * 5,
        out_specs=(hbm,) * 5,
        scratch_shapes=[
            pltpu.VMEM((2, 16, 576), BF16),
            pltpu.VMEM((2, 8, 1152), BF16),
            pltpu.VMEM((2, 3, 576, 576), BF16),
            pltpu.VMEM((2, 576, 1152), BF16),
            pltpu.VMEM((2, 1152, 576), BF16),
            pltpu.VMEM((2, 576, 576), BF16),
            pltpu.VMEM((8, 2, 8, 1152), BF16),
            pltpu.VMEM((8, 2, 8, 1152), BF16),
            pltpu.VMEM((2, 8, 8, 1152), BF16),
            pltpu.VMEM((16, 8, 1152), F32),
            pltpu.VMEM((16, 8, 576), F32),
            pltpu.VMEM((16, 8, 1152), BF16),
            pltpu.VMEM((16, 8, 576), BF16),
            pltpu.VMEM((16, 8, 1152), BF16),
            pltpu.VMEM((16, 8, 576), BF16),
            pltpu.VMEM((16, 8, 576), BF16),
            pltpu.VMEM((16, 8, 1152), BF16),
            pltpu.VMEM((16, 8, 576), BF16),
            pltpu.VMEM((16, 8, 1152), BF16),
            pltpu.VMEM((2, 8, 8, 1152), BF16),
            pltpu.VMEM((2, 8, 8, 1152), BF16),
            pltpu.VMEM((16, 8, 1152), BF16),
            pltpu.VMEM((16, 8, 1152), BF16),
            pltpu.VMEM((2, 16, 576), BF16),
            pltpu.VMEM((3, 576, 576), BF16),
            pltpu.SemaphoreType.REGULAR,
            dma((5,)), dma((5,)),
            dma((3,)), dma((3,)),
            dma((14,)), dma((20,)), dma((14,)), dma((20,)),
            dma((16,)), dma((16,)), dma((16,)), dma((16,)),
            dma((13,)), dma((19,)), dma((13,)), dma((19,)),
            dma((16,)), dma((16,)), dma((16,)), dma((16,)),
            dma((4,)), dma((4,)),
        ],
        compiler_params=pltpu.CompilerParams(
            collective_id=0, has_side_effects=True, vmem_limit_bytes=64 * 1024 * 1024
        ),
        cost_estimate=pl.CostEstimate(
            flops=9 * 2 * 256 * 576 * 576, bytes_accessed=6 * 576 * 576 * 2, transcendentals=8 * 576
        ),
    )(tokens, gate_weight, up_weight, down_weight, cotangent)
    return pl.pallas_call(
        write_back,
        out_shape=(act, act, weight, weight, weight),
        in_specs=[hbm] * 5,
        out_specs=(hbm,) * 5,
        scratch_shapes=[pltpu.VMEM(t.shape, BF16) for t in (act, act, weight, weight, weight)]
        + [dma((11,)), dma((11,))],
        compiler_params=pltpu.CompilerParams(vmem_limit_bytes=64 * 1024 * 1024),
    )(*results)


def solution(mesh):
    placed = (P("gy", "gx"), P("gx", "gy"), P("gx", "gy"), P("gy", "gx"), P("gy", "gx"))
    return jax.shard_map(
        shards,
        mesh=mesh,
        in_specs=placed,
        out_specs=(P("gy", "gx"), P("gy", "gx"), P("gx", "gy"), P("gx", "gy"), P("gy", "gx")),
        check_vma=False,
    )
```

```python
import jax
import jax.numpy as jnp
from jax import lax
from jax.experimental import pallas as pl
from jax.experimental.pallas import tpu as pltpu
from jax.sharding import PartitionSpec as P

MESH = pl.DeviceIdType.MESH
F32 = jnp.float32
BF16 = jnp.bfloat16


def mm(a, b):
    return lax.dot_general(a, b, (((1,), (0,)), ((), ())), preferred_element_type=F32)


def mm_tn(a, b):
    return lax.dot_general(a, b, (((0,), (0,)), ((), ())), preferred_element_type=F32)


def each(start, stop, body):
    def step(i, carry):
        body(i)
        return carry

    lax.fori_loop(start, stop, step, 0)


def kernel(
    tok, wg, wu, wd, cot,
    out, ig, gate_grad, up_grad, down_grad,
    mine, packed, w, wj, wt, wdt, xt, xc, xw, pgu, phg, sgu, shg, rgu, rhg, gh, gd, ghp, gdp, so, si, ro, ri,
    near, lsem, wss, wrs, tss, trs, css, crs, guss, gurs, hgss, hgrs, hss, hrs, dss, drs,
    oss, ors, iss, irs, fss, frs,
):
    gx, gy = lax.axis_index("gx"), lax.axis_index("gy")
    c = gx & 1
    xh, y = gx >> 4, (gx >> 1) & 7
    xl, z = gy >> 3, gy & 7
    other = 1 - c
    me = y * 2 + xh

    def row_dev(dx, dy):
        return (((xh + dx) & 1) * 16 + ((y + dy) & 7) * 2 + c, gy)

    def col_dev(dx, dz, core):
        return (gx - c + core, ((xl + dx) & 1) * 8 + ((z + dz) & 7))

    peer = col_dev(0, 0, other)

    def remote(src, dst, ssem, rsem, dev):
        return pltpu.make_async_remote_copy(
            src_ref=src, dst_ref=dst, send_sem=ssem, recv_sem=rsem, device_id=dev, device_id_type=MESH
        )

    def greet(sem):
        for d in (2, -2, 1, -1, 0):
            for dx in (1, 0):
                devs = [col_dev(dx, d, other)]
                if dx or d:
                    devs += [row_dev(dx, d), col_dev(dx, d, c)]
                for dev in devs:
                    pl.semaphore_signal(sem, inc=1, device_id=dev, device_id_type=MESH)

    barrier = pltpu.get_barrier_semaphore()
    greet(barrier)

    loads = [
        pltpu.make_async_copy(src, dst, lsem.at[n])
        for n, (src, dst) in enumerate(
            [
                (tok, mine.at[0]), (cot, mine.at[1]),
                (wg, w.at[c, 0]), (wu, w.at[c, 1]), (wd, w.at[c, 2]),
            ]
        )
    ]
    for copy in loads:
        copy.start()

    pl.semaphore_wait(barrier, 28)

    loads[0].wait()
    loads[1].wait()
    for n in range(2):
        packed[n] = jnp.concatenate([mine[n, :8], mine[n, 8:]], axis=1)

    def gather(n, dst, ss, rs):
        slot = z * 2 + c

        places = [(dx, d) for d in (2, -2, 1, -1, 0) for dx in (1, 0)]

        def desc(i):
            dx, d = places[i]
            return remote(packed.at[n], dst.at[z, c], ss.at[i], rs.at[slot], col_dev(dx, d, xl))

        def local():
            return pltpu.make_async_copy(packed.at[n], dst.at[z, c], rs.at[slot])

        def start():
            for i in range(9):
                desc(i).start()

            @pl.when(c == xl)
            def _():
                local().start()

            @pl.when(c != xl)
            def _():
                desc(9).start()

        def ahead(side):
            zs = (z - 2 * side) & 7
            k = (1 - side) // 2
            third = remote(dst.at[zs], dst.at[zs], ss.at[10 + k], rs.at[16 + k], col_dev(0, side, c))
            fourth = remote(
                dst.at[zs, k], dst.at[zs, k], ss.at[12 + k], rs.at[18 + k], col_dev(0, 2 * side, c)
            )
            return zs, third, fourth

        def here(zs, k):
            remote(packed.at[n], dst.at[zs, k], ss.at[0], rs.at[zs * 2 + k], peer).wait_recv()

        def forward():
            for side in (1, -1):
                zs, third, fourth = ahead(side)
                here(zs, 0)
                here(zs, 1)
                third.start()
                fourth.start()

        def arrive():
            for d in (0, 1, -1):
                zs = (z + d) & 7
                here(zs, 0)
                here(zs, 1)
            for side in (1, -1):
                _, third, fourth = ahead(side)
                third.wait_recv()
                fourth.wait_recv()

        def finish():
            for i in range(9):
                desc(i).wait_send()

            @pl.when(c != xl)
            def _():
                desc(9).wait_send()

            for side in (1, -1):
                _, third, fourth = ahead(side)
                third.wait_send()
                fourth.wait_send()

        return start, forward, arrive, finish

    tok_start, tok_forward, tok_arrive, tok_finish = gather(0, xt, tss, trs)
    cot_start, cot_forward, cot_arrive, cot_finish = gather(1, xc, css, crs)
    tok_start()
    wcopies = [
        remote(src, w.at[c, n], wss.at[n], wrs.at[n], peer) for n, src in enumerate((wg, wu, wd))
    ]
    for copy in wcopies:
        copy.start()
    greet(near)
    tok_forward()
    cot_start()
    for copy in loads[2:]:
        copy.wait()
    wcopies[0].wait_recv()
    wcopies[1].wait_recv()
    for k in range(2):
        wj[k] = jnp.concatenate([w[k, 0], w[k, 1]], axis=1)
    pl.semaphore_wait(near, 28)

    def rows(x):
        x = x.reshape(64, 1152)
        return jnp.concatenate([x[:, :576], x[:, 576:]], axis=0)

    def shares(x):
        return jnp.concatenate([x[:64], x[64:]], axis=1).reshape(8, 8, 1152)

    def scatter(src, dst, ss, rs):
        def desc(i):
            dx, dy = i & 1, i >> 1
            t = ((y + dy) & 7) * 2 + ((xh + dx) & 1)
            return remote(src.at[t], dst.at[i], ss.at[i], rs.at[i], row_dev(dx, dy))

        return (
            lambda: each(1, 16, lambda i: desc(i).start()),
            lambda: each(1, 16, lambda i: desc(i).wait_recv()),
            lambda: each(1, 16, lambda i: desc(i).wait_send()),
        )

    gu_start, gu_arrive, gu_finish = scatter(sgu, rgu, guss, gurs)
    hg_start, hg_arrive, hg_finish = scatter(shg, rhg, hgss, hgrs)

    tok_arrive()
    p = mm(rows(xt[:, 0]), wj[0]) + mm(rows(xt[:, 1]), wj[1])
    sgu[...] = p.reshape(16, 8, 1152).astype(BF16)
    gu_start()
    pgu[...] = p.reshape(16, 8, 1152)
    cot_forward()
    wcopies[2].wait_recv()
    for k in range(2):
        wdt[k] = w[k, 2].T
    cot_arrive()
    p = mm(rows(xc[:, 0]), wdt[0]) + mm(rows(xc[:, 1]), wdt[1])
    shg[...] = p.reshape(16, 8, 576).astype(BF16)
    hg_start()
    phg[...] = p.reshape(16, 8, 576)
    for k in range(2):
        wt[k] = jnp.concatenate([w[k, 0].T, w[k, 1].T], axis=0)

    fwd = [
        remote(xt.at[:, other], xw.at[0], fss.at[0], frs.at[0], peer),
        remote(xc.at[:, other], xw.at[1], fss.at[1], frs.at[1], peer),
        remote(gh, ghp, fss.at[2], frs.at[2], peer),
        remote(gd, gdp, fss.at[3], frs.at[3], peer),
    ]
    fwd[0].start()
    fwd[1].start()

    def spread(buf, ss, rs):
        places = [(dx, d) for d in (2, -2, 1, -1, 0) for dx in (1, 0)]

        def desc(i):
            return remote(buf.at[me], buf.at[me], ss.at[i], rs.at[me], row_dev(*places[i]))

        def start():
            for i in range(9):
                desc(i).start()

        def pair(dy):
            return pl.ds(pl.multiple_of(((y + dy) & 7) * 2, 2), 2)

        def here(dy):
            ys = (y + dy) & 7
            for k in range(2):
                remote(buf.at[me], buf.at[ys * 2 + k], ss.at[0], rs.at[ys * 2 + k], peer).wait_recv()

        def third(side):
            view = buf.at[pair(-2 * side)]
            k = (1 - side) // 2
            return remote(view, view, ss.at[10 + k], rs.at[16 + k], row_dev(0, side))

        def fourth():
            side = 1 - 2 * c
            view = buf.at[pair(-2 * side)]
            return remote(view, view, ss.at[12], rs.at[18], row_dev(0, 2 * side))

        def forward():
            for side in (1, -1):
                here(-2 * side)
                third(side).start()
            fourth().start()

        def arrive():
            remote(buf.at[me], buf.at[me], ss.at[0], rs.at[y * 2 + 1 - xh], peer).wait_recv()
            here(1)
            here(-1)
            third(1).wait_recv()
            third(-1).wait_recv()
            fourth().wait_recv()

        def finish():
            for i in range(9):
                desc(i).wait_send()
            third(1).wait_send()
            third(-1).wait_send()
            fourth().wait_send()

        return start, forward, arrive, finish

    h_start, h_forward, h_arrive, h_finish = spread(gh, hss, hrs)
    d_start, d_forward, d_arrive, d_finish = spread(gd, dss, drs)

    gu_arrive()
    total = pgu[me]
    for i in range(1, 16):
        total += rgu[i].astype(F32)
    gate, up = total[:, :576], total[:, 576:]
    sig = jax.nn.sigmoid(gate)
    act = gate * sig
    gh[me] = (act * up).astype(BF16)
    h_start()
    slope = up * sig * (1.0 + gate * (1.0 - sig))
    both = jnp.concatenate([slope, act], axis=1)
    hg_arrive()
    hgrad = phg[me]
    for i in range(1, 16):
        hgrad += rhg[i].astype(F32)
    gd[me] = (jnp.concatenate([hgrad, hgrad], axis=1) * both).astype(BF16)
    d_start()
    h_forward()
    d_forward()

    def deliver(src, dst, ss, rs):
        slot = xl * 8 + z

        def desc(k, j):
            zt = (z + j) & 7
            return remote(
                src.at[k, zt], dst.at[slot], ss.at[k * 8 + j], rs.at[slot], (gx - c + k, c * 8 + zt)
            )

        def is_self(k, j):
            return (xl == c) & (c == k) & (j == 0)

        def start(k):
            def one(j):
                @pl.when(is_self(k, j))
                def _():
                    pltpu.make_async_copy(src.at[k, z], dst.at[slot], rs.at[slot]).start()

                @pl.when(jnp.logical_not(is_self(k, j)))
                def _():
                    desc(k, j).start()

            each(0, 8, one)

        def arrive():
            each(
                0, 16, lambda s: remote(src.at[0, 0], dst.at[s], ss.at[0], rs.at[s], peer).wait_recv()
            )

        def finish():
            for k in range(2):

                def one(j):
                    @pl.when(jnp.logical_not(is_self(k, j)))
                    def _():
                        desc(k, j).wait_send()

                each(0, 8, one)

        return start, arrive, finish

    o_start, o_arrive, o_finish = deliver(so, ro, oss, ors)
    i_start, i_arrive, i_finish = deliver(si, ri, iss, irs)

    h_arrive()
    fwd[2].start()
    hidden = gh[...].reshape(128, 576)
    for k in range(2):
        so[k] = shares(mm(hidden, w[k, 2])).astype(BF16)
        o_start(k)
    for copy in fwd[:3]:
        copy.wait_recv()

    def own(x):
        return rows(x[:, pl.ds(c, 1)])

    down_grad[...] = (
        mm_tn(gh[...].reshape(128, 576), own(xc)) + mm_tn(ghp[...].reshape(128, 576), rows(xw[1]))
    ).astype(BF16)

    d_arrive()
    fwd[3].start()
    joined = gd[...].reshape(128, 1152)
    for k in range(2):
        si[k] = shares(mm(joined, wt[k])).astype(BF16)
        i_start(k)
    fwd[3].wait_recv()
    both = mm_tn(own(xt), gd[...].reshape(128, 1152)) + mm_tn(
        rows(xw[0]), gdp[...].reshape(128, 1152)
    )
    gate_grad[...] = both[:, :576].astype(BF16)
    up_grad[...] = both[:, 576:].astype(BF16)

    def summed(ref):
        t = ref[0].astype(F32)
        for s in range(1, 16):
            t += ref[s].astype(F32)
        return jnp.concatenate([t[:, :576], t[:, 576:]], axis=0).astype(BF16)

    o_arrive()
    out[...] = summed(ro)
    for copy in wcopies + fwd:
        copy.wait_send()
    for finish in (tok_finish, cot_finish, gu_finish, hg_finish, h_finish, d_finish, o_finish):
        finish()
    i_arrive()
    ig[...] = summed(ri)
    i_finish()


def write_back(*refs):
    copies = [pltpu.make_async_copy(refs[n], refs[5 + n], refs[10].at[n]) for n in range(5)]
    for copy in copies:
        copy.start()
    for copy in copies:
        copy.wait()


def shards(tokens, gate_weight, up_weight, down_weight, cotangent):
    hbm = pl.BlockSpec(memory_space=pltpu.HBM)
    vmem = pl.BlockSpec(memory_space=pltpu.VMEM)
    dma = pltpu.SemaphoreType.DMA
    act = jax.ShapeDtypeStruct((16, 576), BF16)
    weight = jax.ShapeDtypeStruct((576, 576), BF16)
    results = (act, act, weight, weight, weight)
    held = pl.pallas_call(
        kernel,
        out_shape=tuple(pltpu.VMEM(t.shape, BF16) for t in results),
        in_specs=[hbm] * 5,
        out_specs=(vmem,) * 5,
        scratch_shapes=[
            pltpu.VMEM((2, 16, 576), BF16),
            pltpu.VMEM((2, 8, 1152), BF16),
            pltpu.VMEM((2, 3, 576, 576), BF16),
            pltpu.VMEM((2, 576, 1152), BF16),
            pltpu.VMEM((2, 1152, 576), BF16),
            pltpu.VMEM((2, 576, 576), BF16),
            pltpu.VMEM((8, 2, 8, 1152), BF16),
            pltpu.VMEM((8, 2, 8, 1152), BF16),
            pltpu.VMEM((2, 8, 8, 1152), BF16),
            pltpu.VMEM((16, 8, 1152), F32),
            pltpu.VMEM((16, 8, 576), F32),
            pltpu.VMEM((16, 8, 1152), BF16),
            pltpu.VMEM((16, 8, 576), BF16),
            pltpu.VMEM((16, 8, 1152), BF16),
            pltpu.VMEM((16, 8, 576), BF16),
            pltpu.VMEM((16, 8, 576), BF16),
            pltpu.VMEM((16, 8, 1152), BF16),
            pltpu.VMEM((16, 8, 576), BF16),
            pltpu.VMEM((16, 8, 1152), BF16),
            pltpu.VMEM((2, 8, 8, 1152), BF16),
            pltpu.VMEM((2, 8, 8, 1152), BF16),
            pltpu.VMEM((16, 8, 1152), BF16),
            pltpu.VMEM((16, 8, 1152), BF16),
            pltpu.SemaphoreType.REGULAR,
            dma((5,)),
            dma((3,)), dma((3,)),
            dma((14,)), dma((20,)), dma((14,)), dma((20,)),
            dma((16,)), dma((16,)), dma((16,)), dma((16,)),
            dma((13,)), dma((19,)), dma((13,)), dma((19,)),
            dma((16,)), dma((16,)), dma((16,)), dma((16,)),
            dma((4,)), dma((4,)),
        ],
        compiler_params=pltpu.CompilerParams(
            collective_id=0, has_side_effects=True, vmem_limit_bytes=64_700_000
        ),
        cost_estimate=pl.CostEstimate(
            flops=9 * 2 * 256 * 576 * 576, bytes_accessed=6 * 576 * 576 * 2, transcendentals=8 * 576
        ),
    )(tokens, gate_weight, up_weight, down_weight, cotangent)
    return pl.pallas_call(
        write_back,
        out_shape=results,
        in_specs=[vmem] * 5,
        out_specs=(hbm,) * 5,
        scratch_shapes=[dma((5,))],
        compiler_params=pltpu.CompilerParams(vmem_limit_bytes=4 * 1024 * 1024),
    )(*held)


def solution(mesh):
    placed = (P("gy", "gx"), P("gx", "gy"), P("gx", "gy"), P("gy", "gx"), P("gy", "gx"))
    return jax.shard_map(
        shards,
        mesh=mesh,
        in_specs=placed,
        out_specs=(P("gy", "gx"), P("gy", "gx"), P("gx", "gy"), P("gx", "gy"), P("gy", "gx")),
        check_vma=False,
    )
```

```python
import jax
import jax.numpy as jnp
from jax import lax
from jax.experimental import pallas as pl
from jax.experimental.pallas import tpu as pltpu
from jax.sharding import PartitionSpec as P

MESH = pl.DeviceIdType.MESH
FAR_FIRST = [(d, dx) for d in (4, 3, 5, 2, 6, 1, 7, 0) for dx in (1, 0) if d or dx]
F32 = jnp.float32
BF16 = jnp.bfloat16


def mm(a, b):
    return lax.dot_general(a, b, (((1,), (0,)), ((), ())), preferred_element_type=F32)


def mm_tn(a, b):
    return lax.dot_general(a, b, (((0,), (0,)), ((), ())), preferred_element_type=F32)


def each(start, stop, body):
    def step(i, carry):
        body(i)
        return carry

    lax.fori_loop(start, stop, step, 0)


def kernel(
    tok, wg, wu, wd, cot,
    out, ig, gate_grad, up_grad, down_grad,
    mine, packed, w, wj, wt, wdt, xt, xc, xw, pgu, phg, sgu, shg, rgu, rhg, gh, gd, ghp, gdp, so, si, ro, ri,
    near, lsem, wss, wrs, tss, trs, css, crs, guss, gurs, hgss, hgrs, hss, hrs, dss, drs,
    oss, ors, iss, irs, fss, frs,
):
    gx, gy = lax.axis_index("gx"), lax.axis_index("gy")
    c = gx & 1
    xh, y = gx >> 4, (gx >> 1) & 7
    xl, z = gy >> 3, gy & 7
    other = 1 - c
    me = y * 2 + xh

    def row_dev(dx, dy):
        return (((xh + dx) & 1) * 16 + ((y + dy) & 7) * 2 + c, gy)

    def col_dev(dx, dz, core):
        return (gx - c + core, ((xl + dx) & 1) * 8 + ((z + dz) & 7))

    peer = col_dev(0, 0, other)

    def remote(src, dst, ssem, rsem, dev):
        return pltpu.make_async_remote_copy(
            src_ref=src, dst_ref=dst, send_sem=ssem, recv_sem=rsem, device_id=dev, device_id_type=MESH
        )

    def greet(sem):
        for d in (2, -2, 1, -1, 0):
            for dx in (1, 0):
                devs = [col_dev(dx, d, other)]
                if dx or d:
                    devs += [row_dev(dx, d), col_dev(dx, d, c)]
                for dev in devs:
                    pl.semaphore_signal(sem, inc=1, device_id=dev, device_id_type=MESH)

    barrier = pltpu.get_barrier_semaphore()
    greet(barrier)

    loads = [
        pltpu.make_async_copy(src, dst, lsem.at[n])
        for n, (src, dst) in enumerate(
            [
                (tok, mine.at[0]), (cot, mine.at[1]),
                (wg, w.at[c, 0]), (wu, w.at[c, 1]), (wd, w.at[c, 2]),
            ]
        )
    ]
    for copy in loads:
        copy.start()

    pl.semaphore_wait(barrier, 28)

    loads[0].wait()
    loads[1].wait()
    for n in range(2):
        packed[n] = jnp.concatenate([mine[n, :8], mine[n, 8:]], axis=1)

    def gather(n, dst, ss, rs):
        slot = z * 2 + c

        places = [(dx, d) for d in (2, -2, 1, -1, 0) for dx in (1, 0)]

        def desc(i):
            dx, d = places[i]
            return remote(packed.at[n], dst.at[z, c], ss.at[i], rs.at[slot], col_dev(dx, d, xl))

        def local():
            return pltpu.make_async_copy(packed.at[n], dst.at[z, c], rs.at[slot])

        def start():
            for i in range(9):
                desc(i).start()

            @pl.when(c == xl)
            def _():
                local().start()

            @pl.when(c != xl)
            def _():
                desc(9).start()

        def ahead(side):
            zs = (z - 2 * side) & 7
            k = (1 - side) // 2
            third = remote(dst.at[zs], dst.at[zs], ss.at[10 + k], rs.at[16 + k], col_dev(0, side, c))
            fourth = remote(
                dst.at[zs, k], dst.at[zs, k], ss.at[12 + k], rs.at[18 + k], col_dev(0, 2 * side, c)
            )
            return zs, third, fourth

        def here(zs, k):
            remote(packed.at[n], dst.at[zs, k], ss.at[0], rs.at[zs * 2 + k], peer).wait_recv()

        def forward():
            for side in (1, -1):
                zs, third, fourth = ahead(side)
                here(zs, 0)
                here(zs, 1)
                third.start()
                fourth.start()

        def arrive():
            for d in (0, 1, -1):
                zs = (z + d) & 7
                here(zs, 0)
                here(zs, 1)
            for side in (1, -1):
                _, third, fourth = ahead(side)
                third.wait_recv()
                fourth.wait_recv()

        def finish():
            for i in range(9):
                desc(i).wait_send()

            @pl.when(c != xl)
            def _():
                desc(9).wait_send()

            for side in (1, -1):
                _, third, fourth = ahead(side)
                third.wait_send()
                fourth.wait_send()

        return start, forward, arrive, finish

    tok_start, tok_forward, tok_arrive, tok_finish = gather(0, xt, tss, trs)
    cot_start, cot_forward, cot_arrive, cot_finish = gather(1, xc, css, crs)
    tok_start()
    wcopies = [
        remote(src, w.at[c, n], wss.at[n], wrs.at[n], peer) for n, src in enumerate((wg, wu, wd))
    ]
    for copy in wcopies:
        copy.start()
    greet(near)
    tok_forward()
    cot_start()
    for copy in loads[2:]:
        copy.wait()
    wcopies[0].wait_recv()
    wcopies[1].wait_recv()
    for k in range(2):
        wj[k] = jnp.concatenate([w[k, 0], w[k, 1]], axis=1)
    pl.semaphore_wait(near, 28)

    def rows(x):
        x = x.reshape(64, 1152)
        return jnp.concatenate([x[:, :576], x[:, 576:]], axis=0)

    def shares(x):
        return jnp.concatenate([x[:64], x[64:]], axis=1).reshape(8, 8, 1152)

    def scatter(src, dst, ss, rs):
        def desc(i):
            dx, dy = i & 1, i >> 1
            t = ((y + dy) & 7) * 2 + ((xh + dx) & 1)
            return remote(src.at[t], dst.at[i], ss.at[i], rs.at[i], row_dev(dx, dy))

        return (
            lambda: [desc(d * 2 + dx).start() for d, dx in FAR_FIRST],
            lambda: each(1, 16, lambda i: desc(i).wait_recv()),
            lambda: each(1, 16, lambda i: desc(i).wait_send()),
        )

    gu_start, gu_arrive, gu_finish = scatter(sgu, rgu, guss, gurs)
    hg_start, hg_arrive, hg_finish = scatter(shg, rhg, hgss, hgrs)

    tok_arrive()
    p = mm(rows(xt[:, 0]), wj[0]) + mm(rows(xt[:, 1]), wj[1])
    sgu[...] = p.reshape(16, 8, 1152).astype(BF16)
    gu_start()
    pgu[...] = p.reshape(16, 8, 1152)
    cot_forward()
    wcopies[2].wait_recv()
    for k in range(2):
        wdt[k] = w[k, 2].T
    cot_arrive()
    p = mm(rows(xc[:, 0]), wdt[0]) + mm(rows(xc[:, 1]), wdt[1])
    shg[...] = p.reshape(16, 8, 576).astype(BF16)
    hg_start()
    phg[...] = p.reshape(16, 8, 576)
    for k in range(2):
        wt[k] = jnp.concatenate([w[k, 0].T, w[k, 1].T], axis=0)

    fwd = [
        remote(xt.at[:, other], xw.at[0], fss.at[0], frs.at[0], peer),
        remote(xc.at[:, other], xw.at[1], fss.at[1], frs.at[1], peer),
        remote(gh, ghp, fss.at[2], frs.at[2], peer),
        remote(gd, gdp, fss.at[3], frs.at[3], peer),
    ]
    fwd[0].start()
    fwd[1].start()

    def spread(buf, ss, rs):
        places = [(dx, d) for d in (2, -2, 1, -1, 0) for dx in (1, 0)]

        def desc(i):
            return remote(buf.at[me], buf.at[me], ss.at[i], rs.at[me], row_dev(*places[i]))

        def start():
            for i in range(9):
                desc(i).start()

        def pair(dy):
            return pl.ds(pl.multiple_of(((y + dy) & 7) * 2, 2), 2)

        def here(dy):
            ys = (y + dy) & 7
            for k in range(2):
                remote(buf.at[me], buf.at[ys * 2 + k], ss.at[0], rs.at[ys * 2 + k], peer).wait_recv()

        def third(side):
            view = buf.at[pair(-2 * side)]
            k = (1 - side) // 2
            return remote(view, view, ss.at[10 + k], rs.at[16 + k], row_dev(0, side))

        def fourth():
            side = 1 - 2 * c
            view = buf.at[pair(-2 * side)]
            return remote(view, view, ss.at[12], rs.at[18], row_dev(0, 2 * side))

        def forward():
            for side in (1, -1):
                here(-2 * side)
                third(side).start()
            fourth().start()

        def arrive():
            remote(buf.at[me], buf.at[me], ss.at[0], rs.at[y * 2 + 1 - xh], peer).wait_recv()
            here(1)
            here(-1)
            third(1).wait_recv()
            third(-1).wait_recv()
            fourth().wait_recv()

        def finish():
            for i in range(9):
                desc(i).wait_send()
            third(1).wait_send()
            third(-1).wait_send()
            fourth().wait_send()

        return start, forward, arrive, finish

    def spread_direct(buf, ss, rs):
        def desc(dx, dy):
            return remote(buf.at[me], buf.at[me], ss.at[dy * 2 + dx], rs.at[me], row_dev(dx, dy))

        def here(i):
            t = ((y + (i >> 1)) & 7) * 2 + ((xh + i) & 1)
            remote(buf.at[me], buf.at[t], ss.at[0], rs.at[t], peer).wait_recv()

        return (
            lambda: [desc(dx, dy).start() for dy, dx in FAR_FIRST],
            lambda: each(1, 16, here),
            lambda: [desc(dx, dy).wait_send() for dy, dx in FAR_FIRST],
        )

    h_start, h_arrive, h_finish = spread_direct(gh, hss, hrs)
    d_start, d_forward, d_arrive, d_finish = spread(gd, dss, drs)

    gu_arrive()
    total = pgu[me]
    for i in range(1, 16):
        total += rgu[i].astype(F32)
    gate, up = total[:, :576], total[:, 576:]
    sig = jax.nn.sigmoid(gate)
    act = gate * sig
    gh[me] = (act * up).astype(BF16)
    h_start()
    slope = up * sig * (1.0 + gate * (1.0 - sig))
    both = jnp.concatenate([slope, act], axis=1)
    hg_arrive()
    hgrad = phg[me]
    for i in range(1, 16):
        hgrad += rhg[i].astype(F32)
    gd[me] = (jnp.concatenate([hgrad, hgrad], axis=1) * both).astype(BF16)
    d_start()

    def deliver(src, dst, ss, rs):
        slot = xl * 8 + z

        def desc(k, j):
            zt = (z + j) & 7
            return remote(
                src.at[k, zt], dst.at[slot], ss.at[k * 8 + j], rs.at[slot], (gx - c + k, c * 8 + zt)
            )

        def is_self(k, j):
            return (xl == c) & (c == k) & (j == 0)

        def start(k):
            for j in (4, 3, 5, 2, 6, 1, 7):
                desc(k, j).start()

            @pl.when(is_self(k, 0))
            def _():
                pltpu.make_async_copy(src.at[k, z], dst.at[slot], rs.at[slot]).start()

            @pl.when(jnp.logical_not(is_self(k, 0)))
            def _():
                desc(k, 0).start()

        def arrive():
            each(
                0, 16, lambda s: remote(src.at[0, 0], dst.at[s], ss.at[0], rs.at[s], peer).wait_recv()
            )

        def finish():
            for k in range(2):

                def one(j):
                    @pl.when(jnp.logical_not(is_self(k, j)))
                    def _():
                        desc(k, j).wait_send()

                each(0, 8, one)

        return start, arrive, finish

    o_start, o_arrive, o_finish = deliver(so, ro, oss, ors)
    i_start, i_arrive, i_finish = deliver(si, ri, iss, irs)

    h_arrive()
    fwd[2].start()
    hidden = gh[...].reshape(128, 576)
    for k in range(2):
        so[k] = shares(mm(hidden, w[k, 2])).astype(BF16)
        o_start(k)
    d_forward()
    for copy in fwd[:3]:
        copy.wait_recv()

    def own(x):
        return rows(x[:, pl.ds(c, 1)])

    down_grad[...] = (
        mm_tn(gh[...].reshape(128, 576), own(xc)) + mm_tn(ghp[...].reshape(128, 576), rows(xw[1]))
    ).astype(BF16)

    d_arrive()
    fwd[3].start()
    joined = gd[...].reshape(128, 1152)
    for k in range(2):
        si[k] = shares(mm(joined, wt[k])).astype(BF16)
        i_start(k)
    fwd[3].wait_recv()
    both = mm_tn(own(xt), gd[...].reshape(128, 1152)) + mm_tn(
        rows(xw[0]), gdp[...].reshape(128, 1152)
    )
    gate_grad[...] = both[:, :576].astype(BF16)
    up_grad[...] = both[:, 576:].astype(BF16)

    def summed(ref):
        t = ref[0].astype(F32)
        for s in range(1, 16):
            t += ref[s].astype(F32)
        return jnp.concatenate([t[:, :576], t[:, 576:]], axis=0).astype(BF16)

    o_arrive()
    out[...] = summed(ro)
    for copy in wcopies + fwd:
        copy.wait_send()
    for finish in (tok_finish, cot_finish, gu_finish, hg_finish, h_finish, d_finish, o_finish):
        finish()
    i_arrive()
    ig[...] = summed(ri)
    i_finish()


def write_back(*refs):
    copies = [pltpu.make_async_copy(refs[n], refs[5 + n], refs[10].at[n]) for n in range(5)]
    for copy in copies:
        copy.start()
    for copy in copies:
        copy.wait()


def shards(tokens, gate_weight, up_weight, down_weight, cotangent):
    hbm = pl.BlockSpec(memory_space=pltpu.HBM)
    vmem = pl.BlockSpec(memory_space=pltpu.VMEM)
    dma = pltpu.SemaphoreType.DMA
    act = jax.ShapeDtypeStruct((16, 576), BF16)
    weight = jax.ShapeDtypeStruct((576, 576), BF16)
    results = (act, act, weight, weight, weight)
    held = pl.pallas_call(
        kernel,
        out_shape=tuple(pltpu.VMEM(t.shape, BF16) for t in results),
        in_specs=[hbm] * 5,
        out_specs=(vmem,) * 5,
        scratch_shapes=[
            pltpu.VMEM((2, 16, 576), BF16),
            pltpu.VMEM((2, 8, 1152), BF16),
            pltpu.VMEM((2, 3, 576, 576), BF16),
            pltpu.VMEM((2, 576, 1152), BF16),
            pltpu.VMEM((2, 1152, 576), BF16),
            pltpu.VMEM((2, 576, 576), BF16),
            pltpu.VMEM((8, 2, 8, 1152), BF16),
            pltpu.VMEM((8, 2, 8, 1152), BF16),
            pltpu.VMEM((2, 8, 8, 1152), BF16),
            pltpu.VMEM((16, 8, 1152), F32),
            pltpu.VMEM((16, 8, 576), F32),
            pltpu.VMEM((16, 8, 1152), BF16),
            pltpu.VMEM((16, 8, 576), BF16),
            pltpu.VMEM((16, 8, 1152), BF16),
            pltpu.VMEM((16, 8, 576), BF16),
            pltpu.VMEM((16, 8, 576), BF16),
            pltpu.VMEM((16, 8, 1152), BF16),
            pltpu.VMEM((16, 8, 576), BF16),
            pltpu.VMEM((16, 8, 1152), BF16),
            pltpu.VMEM((2, 8, 8, 1152), BF16),
            pltpu.VMEM((2, 8, 8, 1152), BF16),
            pltpu.VMEM((16, 8, 1152), BF16),
            pltpu.VMEM((16, 8, 1152), BF16),
            pltpu.SemaphoreType.REGULAR,
            dma((5,)),
            dma((3,)), dma((3,)),
            dma((14,)), dma((20,)), dma((14,)), dma((20,)),
            dma((16,)), dma((16,)), dma((16,)), dma((16,)),
            dma((16,)), dma((16,)), dma((13,)), dma((19,)),
            dma((16,)), dma((16,)), dma((16,)), dma((16,)),
            dma((4,)), dma((4,)),
        ],
        compiler_params=pltpu.CompilerParams(
            collective_id=0, has_side_effects=True, vmem_limit_bytes=64_700_000
        ),
        cost_estimate=pl.CostEstimate(
            flops=9 * 2 * 256 * 576 * 576, bytes_accessed=6 * 576 * 576 * 2, transcendentals=8 * 576
        ),
    )(tokens, gate_weight, up_weight, down_weight, cotangent)
    return pl.pallas_call(
        write_back,
        out_shape=results,
        in_specs=[vmem] * 5,
        out_specs=(hbm,) * 5,
        scratch_shapes=[dma((5,))],
        compiler_params=pltpu.CompilerParams(vmem_limit_bytes=4 * 1024 * 1024),
    )(*held)


def solution(mesh):
    placed = (P("gy", "gx"), P("gx", "gy"), P("gx", "gy"), P("gy", "gx"), P("gy", "gx"))
    return jax.shard_map(
        shards,
        mesh=mesh,
        in_specs=placed,
        out_specs=(P("gy", "gx"), P("gy", "gx"), P("gx", "gy"), P("gx", "gy"), P("gy", "gx")),
        check_vma=False,
    )
```

```python
import jax
import jax.numpy as jnp
from jax import lax
from jax.experimental import pallas as pl
from jax.experimental.pallas import tpu as pltpu
from jax.sharding import PartitionSpec as P

MESH = pl.DeviceIdType.MESH
FAR_FIRST = [(d, dx) for d in (4, 3, 5, 2, 6, 1, 7, 0) for dx in (1, 0) if d or dx]
F32 = jnp.float32
BF16 = jnp.bfloat16


def mm(a, b):
    return lax.dot_general(a, b, (((1,), (0,)), ((), ())), preferred_element_type=F32)


def mm_tn(a, b):
    return lax.dot_general(a, b, (((0,), (0,)), ((), ())), preferred_element_type=F32)


def each(start, stop, body):
    def step(i, carry):
        body(i)
        return carry

    lax.fori_loop(start, stop, step, 0)


def kernel(
    tok, wg, wu, wd, cot,
    out, ig, gate_grad, up_grad, down_grad,
    mine, packed, w, wj, wt, wdt, xt, xc, xw, pgu, phg, sgu, shg, rgu, rhg, gh, gd, ghp, gdp, so, si, ro, ri,
    near, lsem, wss, wrs, tss, trs, css, crs, guss, gurs, hgss, hgrs, hss, hrs, dss, drs,
    oss, ors, iss, irs, fss, frs,
):
    gx, gy = lax.axis_index("gx"), lax.axis_index("gy")
    c = gx & 1
    xh, y = gx >> 4, (gx >> 1) & 7
    xl, z = gy >> 3, gy & 7
    other = 1 - c
    me = y * 2 + xh

    def row_dev(dx, dy):
        return (((xh + dx) & 1) * 16 + ((y + dy) & 7) * 2 + c, gy)

    def col_dev(dx, dz, core):
        return (gx - c + core, ((xl + dx) & 1) * 8 + ((z + dz) & 7))

    peer = col_dev(0, 0, other)

    def remote(src, dst, ssem, rsem, dev):
        return pltpu.make_async_remote_copy(
            src_ref=src, dst_ref=dst, send_sem=ssem, recv_sem=rsem, device_id=dev, device_id_type=MESH
        )

    def greet(sem):
        for d in (2, -2, 1, -1, 0):
            for dx in (1, 0):
                devs = [col_dev(dx, d, other)]
                if dx or d:
                    devs += [row_dev(dx, d), col_dev(dx, d, c)]
                for dev in devs:
                    pl.semaphore_signal(sem, inc=1, device_id=dev, device_id_type=MESH)

    barrier = pltpu.get_barrier_semaphore()
    greet(barrier)

    loads = [
        pltpu.make_async_copy(src, dst, lsem.at[n])
        for n, (src, dst) in enumerate(
            [
                (tok, mine.at[0]), (cot, mine.at[1]),
                (wg, w.at[c, 0]), (wu, w.at[c, 1]), (wd, w.at[c, 2]),
            ]
        )
    ]
    for copy in loads:
        copy.start()

    pl.semaphore_wait(barrier, 28)

    loads[0].wait()
    loads[1].wait()
    for n in range(2):
        packed[n] = jnp.concatenate([mine[n, :8], mine[n, 8:]], axis=1)

    def gather(n, dst, ss, rs):
        slot = z * 2 + c

        places = [(dx, d) for d in (2, -2, 1, -1, 0) for dx in (1, 0)]

        def desc(i):
            dx, d = places[i]
            return remote(packed.at[n], dst.at[z, c], ss.at[i], rs.at[slot], col_dev(dx, d, xl))

        def local():
            return pltpu.make_async_copy(packed.at[n], dst.at[z, c], rs.at[slot])

        def start():
            for i in range(9):
                desc(i).start()

            @pl.when(c == xl)
            def _():
                local().start()

            @pl.when(c != xl)
            def _():
                desc(9).start()

        def ahead(side):
            zs = (z - 2 * side) & 7
            k = (1 - side) // 2
            third = remote(dst.at[zs], dst.at[zs], ss.at[10 + k], rs.at[16 + k], col_dev(0, side, c))
            fourth = remote(
                dst.at[zs, k], dst.at[zs, k], ss.at[12 + k], rs.at[18 + k], col_dev(0, 2 * side, c)
            )
            return zs, third, fourth

        def here(zs, k):
            remote(packed.at[n], dst.at[zs, k], ss.at[0], rs.at[zs * 2 + k], peer).wait_recv()

        def forward():
            for side in (1, -1):
                zs, third, fourth = ahead(side)
                here(zs, 0)
                here(zs, 1)
                third.start()
                fourth.start()

        def arrive():
            for d in (0, 1, -1):
                zs = (z + d) & 7
                here(zs, 0)
                here(zs, 1)
            for side in (1, -1):
                _, third, fourth = ahead(side)
                third.wait_recv()
                fourth.wait_recv()

        def finish():
            for i in range(9):
                desc(i).wait_send()

            @pl.when(c != xl)
            def _():
                desc(9).wait_send()

            for side in (1, -1):
                _, third, fourth = ahead(side)
                third.wait_send()
                fourth.wait_send()

        return start, forward, arrive, finish

    tok_start, tok_forward, tok_arrive, tok_finish = gather(0, xt, tss, trs)
    cot_start, cot_forward, cot_arrive, cot_finish = gather(1, xc, css, crs)
    tok_start()
    wcopies = [
        remote(src, w.at[c, n], wss.at[n], wrs.at[n], peer) for n, src in enumerate((wg, wu, wd))
    ]
    for copy in wcopies:
        copy.start()
    greet(near)
    tok_forward()
    cot_start()
    for copy in loads[2:]:
        copy.wait()
    wcopies[0].wait_recv()
    wcopies[1].wait_recv()
    for k in range(2):
        wj[k] = jnp.concatenate([w[k, 0], w[k, 1]], axis=1)
    pl.semaphore_wait(near, 28)

    def rows(x):
        x = x.reshape(64, 1152)
        return jnp.concatenate([x[:, :576], x[:, 576:]], axis=0)

    def shares(x):
        return jnp.concatenate([x[:64], x[64:]], axis=1).reshape(8, 8, 1152)

    def scatter(src, dst, ss, rs):
        def desc(i):
            dx, dy = i & 1, i >> 1
            t = ((y + dy) & 7) * 2 + ((xh + dx) & 1)
            return remote(src.at[t], dst.at[i], ss.at[i], rs.at[i], row_dev(dx, dy))

        return (
            lambda: [desc(d * 2 + dx).start() for d, dx in FAR_FIRST],
            lambda: each(1, 16, lambda i: desc(i).wait_recv()),
            lambda: each(1, 16, lambda i: desc(i).wait_send()),
        )

    gu_start, gu_arrive, gu_finish = scatter(sgu, rgu, guss, gurs)
    hg_start, hg_arrive, hg_finish = scatter(shg, rhg, hgss, hgrs)

    tok_arrive()
    p = mm(rows(xt[:, 0]), wj[0]) + mm(rows(xt[:, 1]), wj[1])
    sgu[...] = p.reshape(16, 8, 1152).astype(BF16)
    gu_start()
    pgu[...] = p.reshape(16, 8, 1152)
    cot_forward()
    wcopies[2].wait_recv()
    for k in range(2):
        wdt[k] = w[k, 2].T
    cot_arrive()
    p = mm(rows(xc[:, 0]), wdt[0]) + mm(rows(xc[:, 1]), wdt[1])
    shg[...] = p.reshape(16, 8, 576).astype(BF16)
    hg_start()
    phg[...] = p.reshape(16, 8, 576)
    for k in range(2):
        wt[k] = jnp.concatenate([w[k, 0].T, w[k, 1].T], axis=0)

    fwd = [
        remote(xt.at[:, other], xw.at[0], fss.at[0], frs.at[0], peer),
        remote(xc.at[:, other], xw.at[1], fss.at[1], frs.at[1], peer),
        remote(gh, ghp, fss.at[2], frs.at[2], peer),
        remote(gd, gdp, fss.at[3], frs.at[3], peer),
    ]
    fwd[0].start()
    fwd[1].start()

    def spread(buf, ss, rs):
        places = [(dx, d) for d in (2, -2, 1, -1, 0) for dx in (1, 0)]

        def desc(i):
            return remote(buf.at[me], buf.at[me], ss.at[i], rs.at[me], row_dev(*places[i]))

        def start():
            for i in range(9):
                desc(i).start()

        def pair(dy):
            return pl.ds(pl.multiple_of(((y + dy) & 7) * 2, 2), 2)

        def here(dy):
            ys = (y + dy) & 7
            for k in range(2):
                remote(buf.at[me], buf.at[ys * 2 + k], ss.at[0], rs.at[ys * 2 + k], peer).wait_recv()

        def third(side):
            view = buf.at[pair(-2 * side)]
            k = (1 - side) // 2
            return remote(view, view, ss.at[10 + k], rs.at[16 + k], row_dev(0, side))

        def fourth():
            side = 1 - 2 * c
            view = buf.at[pair(-2 * side)]
            return remote(view, view, ss.at[12], rs.at[18], row_dev(0, 2 * side))

        def forward():
            for side in (1, -1):
                here(-2 * side)
                third(side).start()
            fourth().start()

        def arrive():
            remote(buf.at[me], buf.at[me], ss.at[0], rs.at[y * 2 + 1 - xh], peer).wait_recv()
            here(1)
            here(-1)
            third(1).wait_recv()
            third(-1).wait_recv()
            fourth().wait_recv()

        def finish():
            for i in range(9):
                desc(i).wait_send()
            third(1).wait_send()
            third(-1).wait_send()
            fourth().wait_send()

        return start, forward, arrive, finish

    def spread_direct(buf, ss, rs):
        def desc(dx, dy):
            return remote(buf.at[me], buf.at[me], ss.at[dy * 2 + dx], rs.at[me], row_dev(dx, dy))

        def here(i):
            t = ((y + (i >> 1)) & 7) * 2 + ((xh + i) & 1)
            remote(buf.at[me], buf.at[t], ss.at[0], rs.at[t], peer).wait_recv()

        return (
            lambda: [desc(dx, dy).start() for dy, dx in FAR_FIRST],
            lambda: each(1, 16, here),
            lambda: [desc(dx, dy).wait_send() for dy, dx in FAR_FIRST],
        )

    h_start, h_arrive, h_finish = spread_direct(gh, hss, hrs)
    d_start, d_arrive, d_finish = spread_direct(gd, dss, drs)

    gu_arrive()
    total = pgu[me]
    for i in range(1, 16):
        total += rgu[i].astype(F32)
    gate, up = total[:, :576], total[:, 576:]
    sig = jax.nn.sigmoid(gate)
    act = gate * sig
    gh[me] = (act * up).astype(BF16)
    h_start()
    slope = up * sig * (1.0 + gate * (1.0 - sig))
    both = jnp.concatenate([slope, act], axis=1)
    hg_arrive()
    hgrad = phg[me]
    for i in range(1, 16):
        hgrad += rhg[i].astype(F32)
    gd[me] = (jnp.concatenate([hgrad, hgrad], axis=1) * both).astype(BF16)
    d_start()

    def deliver(src, dst, ss, rs):
        slot = xl * 8 + z

        def desc(k, j):
            zt = (z + j) & 7
            return remote(
                src.at[k, zt], dst.at[slot], ss.at[k * 8 + j], rs.at[slot], (gx - c + k, c * 8 + zt)
            )

        def is_self(k, j):
            return (xl == c) & (c == k) & (j == 0)

        def start(k):
            for j in (4, 3, 5, 2, 6, 1, 7):
                desc(k, j).start()

            @pl.when(is_self(k, 0))
            def _():
                pltpu.make_async_copy(src.at[k, z], dst.at[slot], rs.at[slot]).start()

            @pl.when(jnp.logical_not(is_self(k, 0)))
            def _():
                desc(k, 0).start()

        def arrive():
            each(
                0, 16, lambda s: remote(src.at[0, 0], dst.at[s], ss.at[0], rs.at[s], peer).wait_recv()
            )

        def finish():
            for k in range(2):

                def one(j):
                    @pl.when(jnp.logical_not(is_self(k, j)))
                    def _():
                        desc(k, j).wait_send()

                each(0, 8, one)

        return start, arrive, finish

    o_start, o_arrive, o_finish = deliver(so, ro, oss, ors)
    i_start, i_arrive, i_finish = deliver(si, ri, iss, irs)

    h_arrive()
    fwd[2].start()
    hidden = gh[...].reshape(128, 576)
    for k in range(2):
        so[k] = shares(mm(hidden, w[k, 2])).astype(BF16)
        o_start(k)
    for copy in fwd[:3]:
        copy.wait_recv()

    def own(x):
        return rows(x[:, pl.ds(c, 1)])

    down_grad[...] = (
        mm_tn(gh[...].reshape(128, 576), own(xc)) + mm_tn(ghp[...].reshape(128, 576), rows(xw[1]))
    ).astype(BF16)

    d_arrive()
    fwd[3].start()
    joined = gd[...].reshape(128, 1152)
    for k in range(2):
        si[k] = shares(mm(joined, wt[k])).astype(BF16)
        i_start(k)
    fwd[3].wait_recv()
    both = mm_tn(own(xt), gd[...].reshape(128, 1152)) + mm_tn(
        rows(xw[0]), gdp[...].reshape(128, 1152)
    )
    gate_grad[...] = both[:, :576].astype(BF16)
    up_grad[...] = both[:, 576:].astype(BF16)

    def summed(ref):
        t = ref[0].astype(F32)
        for s in range(1, 16):
            t += ref[s].astype(F32)
        return jnp.concatenate([t[:, :576], t[:, 576:]], axis=0).astype(BF16)

    o_arrive()
    out[...] = summed(ro)
    for copy in wcopies + fwd:
        copy.wait_send()
    for finish in (tok_finish, cot_finish, gu_finish, hg_finish, h_finish, d_finish, o_finish):
        finish()
    i_arrive()
    ig[...] = summed(ri)
    i_finish()


def write_back(*refs):
    copies = [pltpu.make_async_copy(refs[n], refs[5 + n], refs[10].at[n]) for n in range(5)]
    for copy in copies:
        copy.start()
    for copy in copies:
        copy.wait()


def shards(tokens, gate_weight, up_weight, down_weight, cotangent):
    hbm = pl.BlockSpec(memory_space=pltpu.HBM)
    vmem = pl.BlockSpec(memory_space=pltpu.VMEM)
    dma = pltpu.SemaphoreType.DMA
    act = jax.ShapeDtypeStruct((16, 576), BF16)
    weight = jax.ShapeDtypeStruct((576, 576), BF16)
    results = (act, act, weight, weight, weight)
    held = pl.pallas_call(
        kernel,
        out_shape=tuple(pltpu.VMEM(t.shape, BF16) for t in results),
        in_specs=[hbm] * 5,
        out_specs=(vmem,) * 5,
        scratch_shapes=[
            pltpu.VMEM((2, 16, 576), BF16),
            pltpu.VMEM((2, 8, 1152), BF16),
            pltpu.VMEM((2, 3, 576, 576), BF16),
            pltpu.VMEM((2, 576, 1152), BF16),
            pltpu.VMEM((2, 1152, 576), BF16),
            pltpu.VMEM((2, 576, 576), BF16),
            pltpu.VMEM((8, 2, 8, 1152), BF16),
            pltpu.VMEM((8, 2, 8, 1152), BF16),
            pltpu.VMEM((2, 8, 8, 1152), BF16),
            pltpu.VMEM((16, 8, 1152), F32),
            pltpu.VMEM((16, 8, 576), F32),
            pltpu.VMEM((16, 8, 1152), BF16),
            pltpu.VMEM((16, 8, 576), BF16),
            pltpu.VMEM((16, 8, 1152), BF16),
            pltpu.VMEM((16, 8, 576), BF16),
            pltpu.VMEM((16, 8, 576), BF16),
            pltpu.VMEM((16, 8, 1152), BF16),
            pltpu.VMEM((16, 8, 576), BF16),
            pltpu.VMEM((16, 8, 1152), BF16),
            pltpu.VMEM((2, 8, 8, 1152), BF16),
            pltpu.VMEM((2, 8, 8, 1152), BF16),
            pltpu.VMEM((16, 8, 1152), BF16),
            pltpu.VMEM((16, 8, 1152), BF16),
            pltpu.SemaphoreType.REGULAR,
            dma((5,)),
            dma((3,)), dma((3,)),
            dma((14,)), dma((20,)), dma((14,)), dma((20,)),
            dma((16,)), dma((16,)), dma((16,)), dma((16,)),
            dma((16,)), dma((16,)), dma((16,)), dma((16,)),
            dma((16,)), dma((16,)), dma((16,)), dma((16,)),
            dma((4,)), dma((4,)),
        ],
        compiler_params=pltpu.CompilerParams(
            collective_id=0, has_side_effects=True, vmem_limit_bytes=64_700_000
        ),
        cost_estimate=pl.CostEstimate(
            flops=9 * 2 * 256 * 576 * 576, bytes_accessed=6 * 576 * 576 * 2, transcendentals=8 * 576
        ),
    )(tokens, gate_weight, up_weight, down_weight, cotangent)
    return pl.pallas_call(
        write_back,
        out_shape=results,
        in_specs=[vmem] * 5,
        out_specs=(hbm,) * 5,
        scratch_shapes=[dma((5,))],
        compiler_params=pltpu.CompilerParams(vmem_limit_bytes=4 * 1024 * 1024),
    )(*held)


def solution(mesh):
    placed = (P("gy", "gx"), P("gx", "gy"), P("gx", "gy"), P("gy", "gx"), P("gy", "gx"))
    return jax.shard_map(
        shards,
        mesh=mesh,
        in_specs=placed,
        out_specs=(P("gy", "gx"), P("gy", "gx"), P("gx", "gy"), P("gx", "gy"), P("gy", "gx")),
        check_vma=False,
    )
```
